32 devices in a mesh: gx: 8 (over z, x), gy: 4 (over y, core).
Axes of the slice: x: 2, y: 2, z: 4, core: 2. Of those that a mesh axis runs over, the one named last changes fastest.
Arguments:
- features: bfloat16 [256, 512, 128], P(('gx', 'gy')), may hold values from -6 to 6
- weights: bfloat16 [27, 128, 128], replicated, may hold values from -0.109375 to 0.109375
- cotangent: bfloat16 [256, 512, 128], P(('gx', 'gy')), may hold values from -6 to 6
- occupancy: int32 [256, 512], P(('gx', 'gy')), may hold values 0 or 1
- slot_pos: int32 [256], P(('gx', 'gy')), may hold values from -1 to 15, as said below
Outputs:
- outputs: bfloat16 [256, 512, 128], P(('gx', 'gy'))
- grad_input: bfloat16 [256, 512, 128], P(('gx', 'gy'))
- grad_weight: float32 [27, 128, 128], replicated
The draws below stay inside these ranges and needn't reach their ends.
Inputs may be any that keep to these rules, and one draw needn't show every extreme that they name: `slot_pos`: on each device the 8 slots name distinct positions of its region; live slots come first and the rest hold -1; each device has at least 4 live slots, and some device has all 8 live.
All inputs are finite; a program needn't handle non-finite values. No bound on the sum of `occupancy` on one device may be relied on, other than what follows from the above.
Results may differ from the reference program's by a relative error of at most 0.001.
Values may be sent and summed in bfloat16 or wider, within the bound.
A program may use at most 64 MiB of HBM per device.

```python
import math
import jax
import jax.numpy as jnp
from jax import lax

CHANNELS = 128
BRICK = 8
REGION_X = 4
REGION_Y = 2
REGION_Z = 2
SLOTS = 8
BRICK_VOX = 512
ALL_SLOTS = 256
N_GX = 8
N_GY = 4


def draw_slot_pos(key, part):
    devices = N_GX * N_GY
    positions = REGION_X * REGION_Y * REGION_Z
    count_key = jax.random.fold_in(key, 11)
    full_key = jax.random.fold_in(key, 23)
    order_key = jax.random.fold_in(key, 37)
    counts = jax.random.randint(count_key, (devices,), max(1, SLOTS // 2), SLOTS + 1)
    full_device = jax.random.randint(full_key, (), 0, devices)
    counts = jnp.where(jnp.arange(devices) == full_device, SLOTS, counts)

    def order_one(row_key):
        return jax.random.permutation(row_key, positions)
    orders = jax.vmap(order_one)(jax.random.split(order_key, devices))[:, :SLOTS]
    chosen = jnp.where(jnp.arange(SLOTS)[None, :] < counts[:, None], orders, -1)
    return chosen.reshape(devices * SLOTS).astype(jnp.int32)


def plant(entries, rng, low, top_value):
    dims = entries.shape
    index_at = [jax.random.randint(jax.random.fold_in(rng, axis), (), 0, dims[axis]) for axis in range(len(dims))]
    entries = entries.at[tuple(index_at)].set(low)
    longest = dims.index(max(dims))
    index_at[longest] = (index_at[longest] + 1) % dims[longest]
    return entries.at[tuple(index_at)].set(top_value)


def shard_levels(stream_key, dims, cuts, smallest, largest):
    factor_of, own = 1.0, jax.random.fold_in(stream_key, 6)
    for axis_at, parts in cuts:
        draws = jnp.exp(jax.random.uniform(jax.random.fold_in(own, axis_at), (parts,), jnp.float32, smallest / len(cuts), largest / len(cuts)))
        factor_of = factor_of * jnp.repeat(draws, dims[axis_at] // parts).reshape([-1 if axis == axis_at else 1 for axis in range(len(dims))])
    return factor_of


def scatter_about(key, extent, width, bound, shards=(), held_as=jnp.bfloat16):
    values = width * jax.random.normal(key, extent, jnp.float32)
    if shards:
        values = values * shard_levels(key, extent, shards, -0.22, 0.18)
    return jnp.clip(values, -bound, bound).astype(held_as)


def setup_inputs(seed: int = 0) -> dict:
    key_of = jax.random.split(jax.random.key(seed), 6)
    return {
        "features": scatter_about(key_of[0], (ALL_SLOTS, BRICK_VOX, CHANNELS), 1.0, 6.0, ((0, 32),)),
        "weights": scatter_about(key_of[1], (27, CHANNELS, CHANNELS), (27 * CHANNELS) ** -0.5, 0.109375),
        "cotangent": scatter_about(key_of[2], (ALL_SLOTS, BRICK_VOX, CHANNELS), 1.0, 6.0, ((0, 32),)),
        "occupancy": plant((jax.random.randint(key_of[3], (ALL_SLOTS, BRICK_VOX), 0, 16) < 15).astype(jnp.int32), jax.random.fold_in(key_of[3], 1), 0, 1),
        "slot_pos": draw_slot_pos(jax.random.fold_in(key_of[5], 71), 0),
    }


def offset_list():
    result = []
    for along_x in (-1, 0, 1):
        for along_y in (-1, 0, 1):
            for along_z in (-1, 0, 1):
                result.append((along_x, along_y, along_z))
    return result

def gather_patches(padded, corner, first_offset, offset_count):
    channels = padded.shape[-1]
    block_span = BRICK + 2
    starts = (corner[0], corner[1], corner[2], jnp.zeros((), jnp.int32))
    brick_block = lax.dynamic_slice(padded, starts, (block_span, block_span, block_span, channels))
    columns = []
    for along_x, along_y, along_z in offset_list()[first_offset:first_offset + offset_count]:
        window_cells = brick_block[along_x + 1:along_x + 1 + BRICK, along_y + 1:along_y + 1 + BRICK, along_z + 1:along_z + 1 + BRICK]
        columns.append(window_cells.reshape(BRICK ** 3, channels))
    return jnp.concatenate(columns, axis=1)

def map_grid(values, slot_pos):
    devices = N_GX * N_GY
    positions = REGION_X * REGION_Y * REGION_Z
    channels = values.shape[-1]
    table = jnp.zeros((devices, positions + 1, BRICK ** 3, channels), values.dtype)
    owner = jnp.repeat(jnp.arange(devices, dtype=jnp.int32), SLOTS)
    target = jnp.where(slot_pos >= 0, slot_pos, positions).astype(jnp.int32)
    table = table.at[owner, target].set(values)
    cells = table[:, :positions].reshape(N_GX, N_GY, REGION_X, REGION_Y, REGION_Z, BRICK, BRICK, BRICK, channels)
    cells = cells.transpose(0, 2, 5, 1, 3, 6, 4, 7, 8)
    cells = cells.reshape(N_GX * REGION_X * BRICK, N_GY * REGION_Y * BRICK, REGION_Z * BRICK, channels)
    return jnp.pad(cells, ((1, 1), (1, 1), (1, 1), (0, 0)))

def reference(features, weights, cotangent, occupancy, slot_pos):
    channels = features.shape[-1]
    voxels = BRICK ** 3
    active = (occupancy == 1) & (slot_pos >= 0)[:, None]
    zero_value = jnp.zeros((), features.dtype)
    masked_in = jnp.where(active[:, :, None], features, zero_value)
    masked_cot = jnp.where(active[:, :, None], cotangent, zero_value)
    grid_x = map_grid(masked_in, slot_pos)
    grid_dy = map_grid(masked_cot, slot_pos)
    w_forward = weights.astype(jnp.float32).reshape(27 * channels, channels)
    w_backward = weights[::-1].transpose(0, 2, 1).astype(jnp.float32).reshape(27 * channels, channels)
    highest = lax.Precision.HIGHEST

    def per_slot(slot_index, mask_row, cot_row):
        position = jnp.maximum(slot_pos[slot_index], 0).astype(jnp.int32)
        owner = (slot_index // SLOTS).astype(jnp.int32)
        gx_index = owner // N_GY
        gy_index = owner % N_GY
        corner = ((gx_index * REGION_X + position // (REGION_Y * REGION_Z)) * BRICK, (gy_index * REGION_Y + position // REGION_Z % REGION_Y) * BRICK, position % REGION_Z * BRICK)
        x_patches = gather_patches(grid_x, corner, 0, 27).astype(jnp.float32)
        dy_patches = gather_patches(grid_dy, corner, 0, 27).astype(jnp.float32)
        keep_mask = mask_row.astype(jnp.float32)[:, None]
        result = (jnp.dot(x_patches, w_forward, precision=highest) * keep_mask).astype(jnp.bfloat16)
        grad_in = (jnp.dot(dy_patches, w_backward, precision=highest) * keep_mask).astype(jnp.bfloat16)
        grad_w = jnp.dot(x_patches.T, cot_row.astype(jnp.float32), precision=highest)
        return (result, grad_in, grad_w)
    total_slots = slot_pos.shape[0]
    group_size = math.gcd(total_slots, 16)
    slot_ids = jnp.arange(total_slots, dtype=jnp.int32).reshape(-1, group_size)

    def per_group(pieces):
        results, grads, weight_terms = jax.vmap(per_slot)(pieces[0], pieces[1], pieces[2])
        return (results, grads, lax.optimization_barrier(jnp.sum(weight_terms, axis=0)))
    results, grads, weight_terms = lax.map(per_group, (slot_ids, active.reshape(-1, group_size, voxels), masked_cot.reshape(-1, group_size, voxels, channels)))
    scale = 1.0 / math.sqrt(float(total_slots * voxels))
    grad_weight = (lax.optimization_barrier(jnp.sum(weight_terms, axis=0)) * scale).reshape(27, channels, channels)
    outputs = results.reshape(total_slots, voxels, channels)
    grad_input = grads.reshape(total_slots, voxels, channels)
    return (outputs, grad_input, grad_weight)
```

```python
import functools
import math

import jax
import jax.numpy as jnp
from jax import lax
from jax.experimental import pallas as pl
from jax.experimental.pallas import tpu as pltpu
from jax.sharding import PartitionSpec as P

BRICK = 8
REGION_X = 4
REGION_Y = 2
REGION_Z = 2
FACE = BRICK * BRICK
VMEM_LIMIT = 56 * 1024 * 1024
BF16 = jnp.bfloat16
F32 = jnp.float32


def over_rows(a, b):
    return lax.dot_general(a, b, (((0,), (0,)), ((), ())), preferred_element_type=F32)


def slot_mask(occ_ref, slot):
    slots = occ_ref.shape[0]
    chosen = lax.broadcasted_iota(jnp.int32, (slots, 128), 0) == slot
    on = occ_ref[...].astype(F32)
    return over_rows(on, chosen.astype(F32))


def place_kernel(pos_ref, occ_ref, feat_ref, cot_ref, gx_ref, gd_ref, mc_ref):
    for grid in (gx_ref, gd_ref):
        grid[...] = jnp.zeros_like(grid)

    @pl.loop(0, feat_ref.shape[0])
    def _(slot):
        at = pos_ref[slot]
        keep = slot_mask(occ_ref, slot) * (at >= 0).astype(F32)
        mc = jnp.where(keep > 0.5, cot_ref[slot].astype(F32), 0.0).astype(BF16)
        mx = jnp.where(keep > 0.5, feat_ref[slot].astype(F32), 0.0).astype(BF16)
        mc_ref[slot] = mc

        @pl.when(at >= 0)
        def _():
            bx = at // (REGION_Y * REGION_Z)
            by = at // REGION_Z % REGION_Y
            bz = at % REGION_Z
            rows = pl.ds(pl.multiple_of(by * FACE, FACE), FACE)
            for a in range(BRICK):
                gx_ref[bz, bx * BRICK + a, rows, :] = mx[a * FACE : (a + 1) * FACE]
                gd_ref[bz, bx * BRICK + a, rows, :] = mc[a * FACE : (a + 1) * FACE]


def expand(at, wide, patches):
    at = jnp.maximum(at, 0)
    bx = at // (REGION_Y * REGION_Z)
    by = at // REGION_Z % REGION_Y
    bz = at % REGION_Z
    rows = pl.ds(pl.multiple_of(by * FACE, FACE), FACE + 2 * BRICK)
    spot = lax.broadcasted_iota(jnp.int32, (BRICK + 2, BRICK, 128), 1)
    upper = (bz == 1).astype(F32)
    for x in range(BRICK + 2):
        this = wide[bz, bx * BRICK + x, rows, :].reshape(BRICK + 2, BRICK, 128)
        other = wide[1 - bz, bx * BRICK + x, rows, :].reshape(BRICK + 2, BRICK, 128)
        below = jnp.where(
            spot == 0, pltpu.roll(other, 1, 1) * upper, pltpu.roll(this, 1, 1)
        )
        above = jnp.where(
            spot == BRICK - 1,
            pltpu.roll(other, BRICK - 1, 1) * (1.0 - upper),
            pltpu.roll(this, BRICK - 1, 1),
        )
        for r, moved in enumerate((below, this, above)):
            for q in range(3):
                lanes = slice((q * 3 + r) * 128, (q * 3 + r + 1) * 128)
                patches[x * FACE : (x + 1) * FACE, lanes] = (
                    moved[q : q + BRICK].reshape(FACE, 128).astype(BF16)
                )


def widen(grid, wide):
    @pl.loop(0, grid.shape[1])
    def _(x):
        for bz in range(REGION_Z):
            wide[bz, x] = grid[bz, x].astype(F32)


def wgrad_kernel(scale, pos_ref, gx_ref, mc_ref, out_ref, wide, patches):
    widen(gx_ref, wide)
    out_ref[...] = jnp.zeros_like(out_ref)

    @pl.loop(0, mc_ref.shape[0])
    def _(slot):
        expand(pos_ref[slot], wide, patches)
        for p in range(3):
            part = patches[p * FACE : p * FACE + BRICK * FACE]
            out_ref[p] += over_rows(mc_ref[slot], part) * scale


def conv_kernel(pos_ref, occ_ref, gx_ref, gd_ref, wf_ref, wb_ref, out_ref, gi_ref, wide, patches):
    for grid, weight, result in ((gx_ref, wf_ref, out_ref), (gd_ref, wb_ref, gi_ref)):
        widen(grid, wide)

        @pl.loop(0, result.shape[0])
        def _(slot):
            at = pos_ref[slot]
            expand(at, wide, patches)
            keep = slot_mask(occ_ref, slot) * (at >= 0).astype(F32)
            total = jnp.zeros((BRICK * FACE, 128), F32)
            for p in range(3):
                part = patches[p * FACE : p * FACE + BRICK * FACE]
                total += jnp.dot(part, weight[p], preferred_element_type=F32)
            result[slot] = jnp.where(keep > 0.5, total, 0.0).astype(BF16)


def with_halo(value, sides):
    for axis, dim, width in sides:
        size, length = (lax.axis_size(axis), value.shape[dim])
        up = [(i, (i + 1) % size) for i in range(size - 1)]
        down = [(j, i) for i, j in up]
        last = lax.slice_in_dim(value, length - width, length, axis=dim)
        leading = lax.slice_in_dim(value, 0, width, axis=dim)
        before = lax.ppermute(last, axis, up)
        after = lax.ppermute(leading, axis, down)
        value = jnp.concatenate([before, value, after], axis=dim)
    return value


def shards(features, weights, cotangent, occupancy, slot_pos):
    slots, voxels, channels = features.shape
    devices = lax.axis_size("gx") * lax.axis_size("gy")
    scale = 1.0 / math.sqrt(float(devices * slots * voxels))
    vmem = pl.BlockSpec(memory_space=pltpu.VMEM)
    smem = pl.BlockSpec(memory_space=pltpu.SMEM)
    params = pltpu.CompilerParams(vmem_limit_bytes=VMEM_LIMIT)
    grid_shape = (REGION_Z, REGION_X * BRICK, REGION_Y * FACE, channels)
    wide_shape = (REGION_Z, REGION_X * BRICK + 2, REGION_Y * FACE + 2 * BRICK, channels)
    scratch = [
        pltpu.VMEM(wide_shape, F32),
        pltpu.VMEM(((BRICK + 2) * FACE, 9 * channels), BF16),
    ]
    bricks = jax.ShapeDtypeStruct(features.shape, BF16)

    gx, gd, mc = pl.pallas_call(
        place_kernel,
        out_shape=[jax.ShapeDtypeStruct(grid_shape, BF16)] * 2 + [bricks],
        in_specs=[smem, vmem, vmem, vmem],
        out_specs=[vmem] * 3,
        compiler_params=params,
        name="place",
    )(slot_pos, occupancy, features, cotangent)

    sides = (("gx", 1, 1), ("gy", 2, BRICK))
    gx = with_halo(gx, sides)
    local = pl.pallas_call(
        functools.partial(wgrad_kernel, scale),
        out_shape=jax.ShapeDtypeStruct((3, channels, 9 * channels), F32),
        in_specs=[smem, vmem, vmem],
        out_specs=vmem,
        scratch_shapes=scratch,
        compiler_params=params,
        name="wgrad",
    )(slot_pos, gx, mc)
    summed = lax.psum(local, ("gx", "gy"))
    grad_weight = (
        summed.reshape(3, channels, 9, channels).transpose(0, 2, 3, 1).reshape(27, channels, channels)
    )

    gd = with_halo(gd, sides)
    w_forward = weights.reshape(3, 9 * channels, channels)
    w_backward = weights[::-1].transpose(0, 2, 1).reshape(3, 9 * channels, channels)
    outputs, grad_input = pl.pallas_call(
        conv_kernel,
        out_shape=[bricks, bricks],
        in_specs=[smem] + [vmem] * 5,
        out_specs=[vmem, vmem],
        scratch_shapes=scratch,
        compiler_params=params,
        cost_estimate=pl.CostEstimate(
            flops=4 * slots * voxels * 27 * channels * channels, bytes_accessed=8 << 20, transcendentals=0
        ),
        name="conv",
    )(slot_pos, occupancy, gx, gd, w_forward, w_backward)
    return (outputs, grad_input, grad_weight)


def solution(mesh):
    return jax.shard_map(
        shards,
        mesh=mesh,
        in_specs=(
            P(("gx", "gy"), None, None),
            P(),
            P(("gx", "gy"), None, None),
            P(("gx", "gy"), None),
            P(("gx", "gy")),
        ),
        out_specs=(P(("gx", "gy"), None, None), P(("gx", "gy"), None, None), P()),
        check_vma=False,
    )
```

```python
import functools
import math

import jax
import jax.numpy as jnp
from jax import lax
from jax.experimental import pallas as pl
from jax.experimental.pallas import tpu as pltpu
from jax.sharding import PartitionSpec as P

BRICK = 8
REGION_X = 4
REGION_Y = 2
REGION_Z = 2
FACE = BRICK * BRICK
VMEM_LIMIT = 56 * 1024 * 1024
BF16 = jnp.bfloat16
F32 = jnp.float32


def over_rows(a, b):
    return lax.dot_general(a, b, (((0,), (0,)), ((), ())), preferred_element_type=F32)


def slot_mask(occ_ref, slot):
    slots = occ_ref.shape[0]
    chosen = lax.broadcasted_iota(jnp.int32, (slots, 128), 0) == slot
    on = occ_ref[...].astype(F32)
    return over_rows(on, chosen.astype(F32))


def place_kernel(pos_ref, occ_ref, feat_ref, cot_ref, gx_ref, gd_ref, mc_ref):
    for grid in (gx_ref, gd_ref):
        grid[...] = jnp.zeros_like(grid)

    @pl.loop(0, feat_ref.shape[0])
    def _(slot):
        at = pos_ref[slot]
        keep = slot_mask(occ_ref, slot) * (at >= 0).astype(F32)
        mc = jnp.where(keep > 0.5, cot_ref[slot].astype(F32), 0.0).astype(BF16)
        mx = jnp.where(keep > 0.5, feat_ref[slot].astype(F32), 0.0).astype(BF16)
        mc_ref[slot] = mc

        @pl.when(at >= 0)
        def _():
            bx = at // (REGION_Y * REGION_Z)
            by = at // REGION_Z % REGION_Y
            bz = at % REGION_Z
            rows = pl.ds(pl.multiple_of(by * FACE, FACE), FACE)
            for a in range(BRICK):
                gx_ref[bz, bx * BRICK + a, rows, :] = mx[a * FACE : (a + 1) * FACE]
                gd_ref[bz, bx * BRICK + a, rows, :] = mc[a * FACE : (a + 1) * FACE]


def expand(at, wide, patches):
    at = jnp.maximum(at, 0)
    bx = at // (REGION_Y * REGION_Z)
    by = at // REGION_Z % REGION_Y
    bz = at % REGION_Z
    rows = pl.ds(pl.multiple_of(by * FACE, FACE), FACE + 2 * BRICK)
    spot = lax.broadcasted_iota(jnp.int32, (BRICK + 2, BRICK, 128), 1)
    upper = (bz == 1).astype(F32)
    for x in range(BRICK + 2):
        this = wide[bz, bx * BRICK + x, rows, :].reshape(BRICK + 2, BRICK, 128)
        other = wide[1 - bz, bx * BRICK + x, rows, :].reshape(BRICK + 2, BRICK, 128)
        below = jnp.where(
            spot == 0, pltpu.roll(other, 1, 1) * upper, pltpu.roll(this, 1, 1)
        )
        above = jnp.where(
            spot == BRICK - 1,
            pltpu.roll(other, BRICK - 1, 1) * (1.0 - upper),
            pltpu.roll(this, BRICK - 1, 1),
        )
        for r, moved in enumerate((below, this, above)):
            for q in range(3):
                lanes = slice((q * 3 + r) * 128, (q * 3 + r + 1) * 128)
                patches[x * FACE : (x + 1) * FACE, lanes] = (
                    moved[q : q + BRICK].reshape(FACE, 128).astype(BF16)
                )


def widen(grid, wide):
    @pl.loop(0, grid.shape[1])
    def _(x):
        for bz in range(REGION_Z):
            wide[bz, x] = grid[bz, x].astype(F32)


def wgrad_kernel(scale, pos_ref, gx_ref, mc_ref, out_ref, wide, patches):
    widen(gx_ref, wide)
    out_ref[...] = jnp.zeros_like(out_ref)

    @pl.loop(0, mc_ref.shape[0])
    def _(slot):
        expand(pos_ref[slot], wide, patches)
        for p in range(3):
            part = patches[p * FACE : p * FACE + BRICK * FACE]
            out_ref[p] += over_rows(mc_ref[slot], part) * scale


def conv_kernel(pos_ref, occ_ref, gx_ref, gd_ref, wf_ref, wb_ref, out_ref, gi_ref, wide, patches):
    for grid, weight, result in ((gx_ref, wf_ref, out_ref), (gd_ref, wb_ref, gi_ref)):
        widen(grid, wide)

        @pl.loop(0, result.shape[0])
        def _(slot):
            at = pos_ref[slot]
            expand(at, wide, patches)
            keep = slot_mask(occ_ref, slot) * (at >= 0).astype(F32)
            total = jnp.zeros((BRICK * FACE, 128), F32)
            for p in range(3):
                part = patches[p * FACE : p * FACE + BRICK * FACE]
                total += jnp.dot(part, weight[p], preferred_element_type=F32)
            result[slot] = jnp.where(keep > 0.5, total, 0.0).astype(BF16)


def with_halo(value, sides):
    for axis, dim, width in sides:
        size, length = (lax.axis_size(axis), value.shape[dim])
        up = [(i, (i + 1) % size) for i in range(size - 1)]
        down = [(j, i) for i, j in up]
        last = lax.slice_in_dim(value, length - width, length, axis=dim)
        leading = lax.slice_in_dim(value, 0, width, axis=dim)
        before = lax.ppermute(last, axis, up)
        after = lax.ppermute(leading, axis, down)
        value = jnp.concatenate([before, value, after], axis=dim)
    return value


def total_over(value, steps):
    sent = []
    for axis, stride in steps:
        size = lax.axis_size(axis)
        pairs = [(i, i ^ stride) for i in range(size)]
        bit = (lax.axis_index(axis) // stride) % 2
        half = value.shape[0] // 2
        mine = lax.dynamic_slice_in_dim(value, bit * half, half, axis=0)
        other = lax.dynamic_slice_in_dim(value, (1 - bit) * half, half, axis=0)
        value = mine + lax.ppermute(other, axis, pairs)
        sent.append((axis, pairs, bit))
    for axis, pairs, bit in reversed(sent):
        other = lax.ppermute(value, axis, pairs)
        low = jnp.where(bit == 0, value, other)
        high = jnp.where(bit == 0, other, value)
        value = jnp.concatenate([low, high], axis=0)
    return value


def axis_steps(axis):
    return [(axis, 1 << k) for k in range(lax.axis_size(axis).bit_length() - 1)]


def all_sum(value):
    rows = value.shape[0]
    unit = 2 * 8 * lax.axis_size("gx") * lax.axis_size("gy")
    padded = -(-rows // unit) * unit
    value = jnp.pad(value, ((0, padded - rows), (0, 0)))
    along_x, along_y = axis_steps("gx"), axis_steps("gy")
    first = total_over(value[: padded // 2], along_y + along_x)
    second = total_over(value[padded // 2 :], along_y[:1] + along_x + along_y[1:])
    return jnp.concatenate([first, second], axis=0)[:rows]


def shards(features, weights, cotangent, occupancy, slot_pos):
    slots, voxels, channels = features.shape
    devices = lax.axis_size("gx") * lax.axis_size("gy")
    scale = 1.0 / math.sqrt(float(devices * slots * voxels))
    vmem = pl.BlockSpec(memory_space=pltpu.VMEM)
    smem = pl.BlockSpec(memory_space=pltpu.SMEM)
    params = pltpu.CompilerParams(vmem_limit_bytes=VMEM_LIMIT)
    grid_shape = (REGION_Z, REGION_X * BRICK, REGION_Y * FACE, channels)
    wide_shape = (REGION_Z, REGION_X * BRICK + 2, REGION_Y * FACE + 2 * BRICK, channels)
    scratch = [
        pltpu.VMEM(wide_shape, F32),
        pltpu.VMEM(((BRICK + 2) * FACE, 9 * channels), BF16),
    ]
    bricks = jax.ShapeDtypeStruct(features.shape, BF16)

    gx, gd, mc = pl.pallas_call(
        place_kernel,
        out_shape=[jax.ShapeDtypeStruct(grid_shape, BF16)] * 2 + [bricks],
        in_specs=[smem, vmem, vmem, vmem],
        out_specs=[vmem] * 3,
        compiler_params=params,
        name="place",
    )(slot_pos, occupancy, features, cotangent)

    sides = (("gx", 1, 1), ("gy", 2, BRICK))
    gx = with_halo(gx, sides)
    local = pl.pallas_call(
        functools.partial(wgrad_kernel, scale),
        out_shape=jax.ShapeDtypeStruct((3, channels, 9 * channels), F32),
        in_specs=[smem, vmem, vmem],
        out_specs=vmem,
        scratch_shapes=scratch,
        compiler_params=params,
        name="wgrad",
    )(slot_pos, gx, mc)
    local = local.reshape(3, channels, 9, channels).transpose(0, 2, 3, 1)
    summed = all_sum(local.reshape(27 * channels, channels))
    grad_weight = summed.reshape(27, channels, channels)

    gd = with_halo(gd, sides)
    w_forward = weights.reshape(3, 9 * channels, channels)
    w_backward = weights[::-1].transpose(0, 2, 1).reshape(3, 9 * channels, channels)
    outputs, grad_input = pl.pallas_call(
        conv_kernel,
        out_shape=[bricks, bricks],
        in_specs=[smem] + [vmem] * 5,
        out_specs=[vmem, vmem],
        scratch_shapes=scratch,
        compiler_params=params,
        cost_estimate=pl.CostEstimate(
            flops=4 * slots * voxels * 27 * channels * channels, bytes_accessed=8 << 20, transcendentals=0
        ),
        name="conv",
    )(slot_pos, occupancy, gx, gd, w_forward, w_backward)
    return (outputs, grad_input, grad_weight)


def solution(mesh):
    return jax.shard_map(
        shards,
        mesh=mesh,
        in_specs=(
            P(("gx", "gy"), None, None),
            P(),
            P(("gx", "gy"), None, None),
            P(("gx", "gy"), None),
            P(("gx", "gy")),
        ),
        out_specs=(P(("gx", "gy"), None, None), P(("gx", "gy"), None, None), P()),
        check_vma=False,
    )
```

```python
import functools
import math

import jax
import jax.numpy as jnp
from jax import lax
from jax.experimental import pallas as pl
from jax.experimental.pallas import tpu as pltpu
from jax.sharding import PartitionSpec as P

BRICK = 8
REGION_X = 4
REGION_Y = 2
REGION_Z = 2
FACE = BRICK * BRICK
VMEM_LIMIT = 56 * 1024 * 1024
BF16 = jnp.bfloat16
F32 = jnp.float32


def over_rows(a, b):
    return lax.dot_general(a, b, (((0,), (0,)), ((), ())), preferred_element_type=F32)


def slot_mask(occ_ref, slot):
    slots = occ_ref.shape[0]
    chosen = lax.broadcasted_iota(jnp.int32, (slots, 128), 0) == slot
    on = occ_ref[...].astype(F32)
    return over_rows(on, chosen.astype(F32))


def place_kernel(pos_ref, occ_ref, feat_ref, cot_ref, grids_ref, mc_ref):
    grids_ref[...] = jnp.zeros_like(grids_ref)

    @pl.loop(0, feat_ref.shape[0])
    def _(slot):
        at = pos_ref[slot]
        keep = slot_mask(occ_ref, slot) * (at >= 0).astype(F32)
        mc = jnp.where(keep > 0.5, cot_ref[slot].astype(F32), 0.0).astype(BF16)
        mx = jnp.where(keep > 0.5, feat_ref[slot].astype(F32), 0.0).astype(BF16)
        mc_ref[slot] = mc

        @pl.when(at >= 0)
        def _():
            bx = at // (REGION_Y * REGION_Z)
            by = at // REGION_Z % REGION_Y
            bz = at % REGION_Z
            rows = pl.ds(pl.multiple_of(by * FACE, FACE), FACE)
            for a in range(BRICK):
                grids_ref[bz, bx * BRICK + a, rows, :] = mx[a * FACE : (a + 1) * FACE]
                grids_ref[REGION_Z + bz, bx * BRICK + a, rows, :] = mc[a * FACE : (a + 1) * FACE]


def expand(at, wide, patches):
    at = jnp.maximum(at, 0)
    bx = at // (REGION_Y * REGION_Z)
    by = at // REGION_Z % REGION_Y
    bz = at % REGION_Z
    rows = pl.ds(pl.multiple_of(by * FACE, FACE), FACE + 2 * BRICK)
    spot = lax.broadcasted_iota(jnp.int32, (BRICK + 2, BRICK, 128), 1)
    upper = (bz == 1).astype(F32)
    for x in range(BRICK + 2):
        this = wide[bz, bx * BRICK + x, rows, :].reshape(BRICK + 2, BRICK, 128)
        other = wide[1 - bz, bx * BRICK + x, rows, :].reshape(BRICK + 2, BRICK, 128)
        below = jnp.where(
            spot == 0, pltpu.roll(other, 1, 1) * upper, pltpu.roll(this, 1, 1)
        )
        above = jnp.where(
            spot == BRICK - 1,
            pltpu.roll(other, BRICK - 1, 1) * (1.0 - upper),
            pltpu.roll(this, BRICK - 1, 1),
        )
        for r, moved in enumerate((below, this, above)):
            for q in range(3):
                lanes = slice((q * 3 + r) * 128, (q * 3 + r + 1) * 128)
                patches[x * FACE : (x + 1) * FACE, lanes] = (
                    moved[q : q + BRICK].reshape(FACE, 128).astype(BF16)
                )


def widen(grid, wide):
    @pl.loop(0, grid.shape[1])
    def _(x):
        for bz in range(REGION_Z):
            wide[bz, x] = grid[bz, x].astype(F32)


def wgrad_kernel(scale, pos_ref, gx_ref, mc_ref, out_ref, wide, patches):
    widen(gx_ref, wide)
    out_ref[...] = jnp.zeros_like(out_ref)

    @pl.loop(0, mc_ref.shape[0])
    def _(slot):
        expand(pos_ref[slot], wide, patches)
        for p in range(3):
            part = patches[p * FACE : p * FACE + BRICK * FACE]
            out_ref[p] += over_rows(mc_ref[slot], part) * scale


def conv_kernel(pos_ref, occ_ref, grid_ref, weight_ref, result_ref, wide, patches):
    widen(grid_ref, wide)

    @pl.loop(0, result_ref.shape[0])
    def _(slot):
        at = pos_ref[slot]
        expand(at, wide, patches)
        keep = slot_mask(occ_ref, slot) * (at >= 0).astype(F32)
        total = jnp.zeros((BRICK * FACE, 128), F32)
        for p in range(3):
            part = patches[p * FACE : p * FACE + BRICK * FACE]
            total += jnp.dot(part, weight_ref[p], preferred_element_type=F32)
        result_ref[slot] = jnp.where(keep > 0.5, total, 0.0).astype(BF16)


def with_halo(value, sides):
    for axis, dim, width in sides:
        size, length = (lax.axis_size(axis), value.shape[dim])
        up = [(i, (i + 1) % size) for i in range(size - 1)]
        down = [(j, i) for i, j in up]
        last = lax.slice_in_dim(value, length - width, length, axis=dim)
        leading = lax.slice_in_dim(value, 0, width, axis=dim)
        before = lax.ppermute(last, axis, up)
        after = lax.ppermute(leading, axis, down)
        value = jnp.concatenate([before, value, after], axis=dim)
    return value


def halve(value, step):
    axis, stride = step
    pairs = [(i, i ^ stride) for i in range(lax.axis_size(axis))]
    bit = (lax.axis_index(axis) // stride) % 2
    half = value.shape[0] // 2
    mine = lax.dynamic_slice_in_dim(value, bit * half, half, axis=0)
    other = lax.dynamic_slice_in_dim(value, (1 - bit) * half, half, axis=0)
    return mine, lax.ppermute(other, axis, pairs)


def double(value, step):
    axis, stride = step
    pairs = [(i, i ^ stride) for i in range(lax.axis_size(axis))]
    bit = (lax.axis_index(axis) // stride) % 2
    other = lax.ppermute(value, axis, pairs)
    low = jnp.where(bit == 0, value, other)
    high = jnp.where(bit == 0, other, value)
    return jnp.concatenate([low, high], axis=0)


def axis_steps(axis):
    return [(axis, 1 << k) for k in range(lax.axis_size(axis).bit_length() - 1)]


def all_sum(value, beside):
    rows = value.shape[0]
    unit = 2 * 8 * lax.axis_size("gx") * lax.axis_size("gy")
    padded = -(-rows // unit) * unit
    value = jnp.pad(value, ((0, padded - rows), (0, 0)))
    along_x, along_y = axis_steps("gx"), axis_steps("gy")
    orders = (along_y + along_x, along_y[:1] + along_x + along_y[1:])
    parts = [value[: padded // 2], value[padded // 2 :]]
    made = list(beside)
    for number, steps in enumerate(zip(*orders)):
        pairs = [halve(part, step) for part, step in zip(parts, steps)]
        if number < len(made):
            a, b, made[number] = lax.optimization_barrier((pairs[0][0], pairs[1][0], made[number]))
            pairs = [(a, pairs[0][1]), (b, pairs[1][1])]
        parts = [mine + other for mine, other in pairs]
    for steps in reversed(list(zip(*orders))):
        parts = [double(part, step) for part, step in zip(parts, steps)]
    return jnp.concatenate(parts, axis=0)[:rows], made


def shards(features, weights, cotangent, occupancy, slot_pos):
    slots, voxels, channels = features.shape
    devices = lax.axis_size("gx") * lax.axis_size("gy")
    scale = 1.0 / math.sqrt(float(devices * slots * voxels))
    vmem = pl.BlockSpec(memory_space=pltpu.VMEM)
    smem = pl.BlockSpec(memory_space=pltpu.SMEM)
    params = pltpu.CompilerParams(vmem_limit_bytes=VMEM_LIMIT)
    grid_shape = (2 * REGION_Z, REGION_X * BRICK, REGION_Y * FACE, channels)
    wide_shape = (REGION_Z, REGION_X * BRICK + 2, REGION_Y * FACE + 2 * BRICK, channels)
    scratch = [
        pltpu.VMEM(wide_shape, F32),
        pltpu.VMEM(((BRICK + 2) * FACE, 9 * channels), BF16),
    ]
    bricks = jax.ShapeDtypeStruct(features.shape, BF16)

    grids, mc = pl.pallas_call(
        place_kernel,
        out_shape=[jax.ShapeDtypeStruct(grid_shape, BF16), bricks],
        in_specs=[smem, vmem, vmem, vmem],
        out_specs=[vmem] * 2,
        compiler_params=params,
        name="place",
    )(slot_pos, occupancy, features, cotangent)
    grids = with_halo(grids, (("gx", 1, 1), ("gy", 2, BRICK)))

    def grid_spec(which):
        return pl.BlockSpec(wide_shape, lambda i: (which, 0, 0, 0))

    local = pl.pallas_call(
        functools.partial(wgrad_kernel, scale),
        grid=(1,),
        out_shape=jax.ShapeDtypeStruct((3, channels, 9 * channels), F32),
        in_specs=[smem, grid_spec(0), vmem],
        out_specs=vmem,
        scratch_shapes=scratch,
        compiler_params=params,
        name="wgrad",
    )(slot_pos, grids, mc)
    local = local.reshape(3, channels, 9, channels).transpose(0, 2, 3, 1)

    def conv(which, weight, name):
        return pl.pallas_call(
            conv_kernel,
            grid=(1,),
            out_shape=bricks,
            in_specs=[smem, vmem, grid_spec(which), vmem],
            out_specs=vmem,
            scratch_shapes=scratch,
            compiler_params=params,
            cost_estimate=pl.CostEstimate(
                flops=2 * slots * voxels * 27 * channels * channels,
                bytes_accessed=4 << 20,
                transcendentals=0,
            ),
            name=name,
        )(slot_pos, occupancy, grids, weight)

    outputs = conv(0, weights.reshape(3, 9 * channels, channels), "forward")
    w_backward = weights[::-1].transpose(0, 2, 1).reshape(3, 9 * channels, channels)
    grad_input = conv(1, w_backward, "input_grad")
    summed, (outputs, grad_input) = all_sum(local.reshape(27 * channels, channels), (outputs, grad_input))
    grad_weight = summed.reshape(27, channels, channels)
    return (outputs, grad_input, grad_weight)


def solution(mesh):
    return jax.shard_map(
        shards,
        mesh=mesh,
        in_specs=(
            P(("gx", "gy"), None, None),
            P(),
            P(("gx", "gy"), None, None),
            P(("gx", "gy"), None),
            P(("gx", "gy")),
        ),
        out_specs=(P(("gx", "gy"), None, None), P(("gx", "gy"), None, None), P()),
        check_vma=False,
    )
```
